32 devices in a mesh: section: 4 (over x, core), blk: 8 (over z, y).
Axes of the slice: x: 2, y: 2, z: 4, core: 2. Of those that a mesh axis runs over, the one named last changes fastest.
Arguments:
- features: bfloat16 [4, 4096, 256], P(None, 'blk'), may hold values from -6 to 6
- tile_values: bfloat16 [4, 640, 128, 128], P(None, 'blk'), may hold values from -1 to 1
- tile_rows: int32 [4, 640], P(None, 'blk'), may hold values from 0 to 31, as said below
- tile_cols: int32 [4, 640], P(None, 'blk'), may hold values from 0 to 31, as said below
- tile_count: int32 [4, 8], P(None, 'blk'), may hold values from 10 to 80, as said below
- degrees: int32 [4, 4096], P(None, 'blk'), may hold values from 16 to 64
- self_weight: bfloat16 [4, 256, 256], P('section'), may hold values from -0.375 to 0.375
- neighbour_weight: bfloat16 [4, 256, 256], P('section'), may hold values from -0.375 to 0.375
Outputs:
- layer_outputs: bfloat16 [4, 4, 4096, 256], P('section', None, 'blk')
The draws below stay inside these ranges and needn't reach their ends.
Inputs may be any that keep to these rules, and one draw needn't show every extreme that they name: `tile_rows`: slot k names a row block of its own blk index: between 4 * (k div 80) and 4 * (k div 80) + 3. `tile_cols`: slot k names a column block of a blk index at most 2 away from k div 80, counting around the axis; the 80 slots of one blk index name distinct row and column block pairs. `tile_count`: in every batch some blk index has all 80 slots live.
All inputs are finite; a program needn't handle non-finite values.
Results may differ from the reference program's by a relative error of at most 0.017.
Values may be sent and summed in bfloat16 or wider, within the bound.
A program may use at most 64 MiB of HBM per device.

```python
import jax
import jax.numpy as jnp
from jax import lax

F = 256
BLOCK = 128
REACH = 2
NB_DEV = 4
BATCHES = 4
TMAX = 80
SLOTS = 640
NBLOCKS = 32
NODES = 4096
LAYERS = 4
N_BLK = 8


def tile_layout(key):
    devices = NBLOCKS // NB_DEV
    band = (2 * REACH + 1) * NB_DEV
    scores = jax.random.randint(jax.random.fold_in(key, 11), (BATCHES, devices, TMAX), 0, 1 << 20)
    scores = scores * TMAX + jnp.arange(TMAX, dtype=jnp.int32)
    ordering = jnp.argsort(scores, axis=-1).astype(jnp.int32)
    local_row = ordering // band
    remainder = ordering % band
    offset = remainder // NB_DEV - REACH
    column_part = remainder % NB_DEV
    owners = jnp.arange(devices, dtype=jnp.int32)[None, :, None]
    rows = owners * NB_DEV + local_row
    cols = jnp.mod(owners + offset, devices) * NB_DEV + column_part
    return (rows.reshape(BATCHES, SLOTS).astype(jnp.int32), cols.reshape(BATCHES, SLOTS).astype(jnp.int32))


def draw_tile_rows(key, part):
    return tile_layout(key)[0]


def draw_tile_cols(key, part):
    return tile_layout(key)[1]


def draw_tile_count(key, part):
    devices = NBLOCKS // NB_DEV
    lowest = max(1, TMAX // 8)
    spread = TMAX - lowest
    first = jax.random.randint(jax.random.fold_in(key, 3), (BATCHES, devices), 0, spread + 1)
    second = jax.random.randint(jax.random.fold_in(key, 5), (BATCHES, devices), 0, spread + 1)
    counts = lowest + first * second // spread
    busiest = jax.random.randint(jax.random.fold_in(key, 9), (BATCHES, 1), 0, devices)
    counts = jnp.where(jnp.arange(devices, dtype=jnp.int32)[None, :] == busiest, TMAX, counts)
    return counts.astype(jnp.int32)


def place_ends(values, rng, least, high):
    extent = values.shape
    spot = [jax.random.randint(jax.random.fold_in(rng, axis), (), 0, extent[axis]) for axis in range(len(extent))]
    values = values.at[tuple(spot)].set(least)
    longest = extent.index(max(extent))
    spot[longest] = (spot[longest] + 1) % extent[longest]
    return values.at[tuple(spot)].set(high)


def block_levels(stream_key, extent, cuts, low, largest):
    def one(position, blocks):
        heights = jax.random.uniform(jax.random.fold_in(jax.random.fold_in(stream_key, 6), position), (blocks,), jnp.float32, low / len(cuts), largest / len(cuts))
        return jnp.repeat(jnp.exp(heights), extent[position] // blocks).reshape((-1,) + (1,) * (len(extent) - position - 1))

    gain = one(*cuts[0])
    for cut in cuts[1:]:
        gain = gain * one(*cut)
    return gain


def bell_draw(key, dims, deviation, reach, split=(), kind=jnp.bfloat16):
    values = deviation * jax.random.normal(key, dims, jnp.float32)
    if split:
        values = values * block_levels(key, dims, split, -0.22, 0.18)
    return jnp.clip(values, -reach, reach).astype(kind)


def setup_inputs(seed: int = 0) -> dict:
    seeds = jax.random.split(jax.random.key(seed), 9)
    return {
        "features": bell_draw(seeds[0], (BATCHES, NODES, F), 1.0, 6.0, ((1, 8),)),
        "tile_values": jnp.clip(jax.random.uniform(seeds[1], (BATCHES, SLOTS, BLOCK, BLOCK), jnp.float32, -1.0, 1.0) * block_levels(seeds[1], (BATCHES, SLOTS, BLOCK, BLOCK), ((1, 8),), -0.4, 0.0), -1.0, 1.0).astype(jnp.bfloat16),
        "tile_rows": draw_tile_rows(jax.random.fold_in(seeds[8], 71), 0),
        "tile_cols": draw_tile_cols(jax.random.fold_in(seeds[8], 71), 0),
        "tile_count": draw_tile_count(jax.random.fold_in(seeds[8], 71), 0),
        "degrees": place_ends(jax.random.randint(seeds[5], (BATCHES, NODES), 16, 65), jax.random.fold_in(seeds[5], 1), 16, 64).astype(jnp.int32),
        "self_weight": bell_draw(seeds[6], (LAYERS, F, F), F ** -0.5, 0.375, ((0, 4),)),
        "neighbour_weight": bell_draw(seeds[7], (LAYERS, F, F), F ** -0.5, 0.375, ((0, 4),)),
    }


def node_layer(hidden, values, rows, cols, count, degree, self_matrix, neighbour_matrix):
    blocks = hidden.reshape(NBLOCKS, BLOCK, F)

    def group_sum(group_args):
        group_values, group_rows, group_cols, group_count, owners = group_args
        gathered = blocks[group_cols].astype(jnp.float32)
        product = jnp.einsum('kij,kjf->kif', group_values.astype(jnp.float32), gathered)
        alive = jnp.arange(TMAX, dtype=jnp.int32) < group_count
        local_rows = group_rows - owners * NB_DEV
        select = ((local_rows[None, :] == jnp.arange(NB_DEV, dtype=jnp.int32)[:, None]) & alive[None, :]).astype(jnp.float32)
        return jnp.einsum('rk,kif->rif', select, product)
    sums = lax.map(group_sum, (values.reshape(N_BLK, TMAX, BLOCK, BLOCK), rows.reshape(N_BLK, TMAX), cols.reshape(N_BLK, TMAX), count, jnp.arange(N_BLK, dtype=jnp.int32)))
    summed = sums.reshape(NODES, F)
    neighbour_mean = (summed / degree.astype(jnp.float32)[:, None]).astype(jnp.bfloat16)
    combined = jnp.dot(hidden, self_matrix, preferred_element_type=jnp.float32) + jnp.dot(neighbour_mean, neighbour_matrix, preferred_element_type=jnp.float32)
    active = jnp.maximum(combined, 0.0)
    scale = lax.rsqrt(lax.optimization_barrier(jnp.mean(active * active, axis=-1, keepdims=True)) + 1e-05)
    return (active * scale).astype(jnp.bfloat16)

def reference(features, tile_values, tile_rows, tile_cols, tile_count, degrees, self_weight, neighbour_weight):
    results = []
    for batch in range(BATCHES):
        hidden = features[batch]
        per_layer = []
        for level in range(LAYERS):
            hidden = node_layer(hidden, tile_values[batch], tile_rows[batch], tile_cols[batch], tile_count[batch], degrees[batch], self_weight[level], neighbour_weight[level])
            per_layer.append(hidden)
        results.append(jnp.stack(per_layer))
    return jnp.stack(results, axis=1)
```

```python
import functools

import jax
import jax.numpy as jnp
from jax import lax
from jax.experimental import pallas as pl
from jax.experimental.pallas import tpu as pltpu
from jax.sharding import PartitionSpec as P

REACH = 2
SPAN = 2 * REACH + 1
MESH = pl.DeviceIdType.MESH


def kernel(
    sections, peers, batches, blocks, chunks,
    slot_ref, deg_ref, feat_ref, vals_ref, ws_ref, wn_ref, out_ref,
    tiles, slab, win, wbuf, acc, own_part, rdeg,
    local_sem, send_sem, recv_sem, fwd_sem, wsend_sem, wrecv_sem, osend_sem, orecv_sem,
):
    section = lax.axis_index("section")
    me = lax.axis_index("blk")
    group = sections // batches
    batch = section // group
    odd = lax.rem(me, 2)
    peer = me + 1 - 2 * odd
    up = lax.rem(me + 2, peers)
    down = lax.rem(me + peers - 2, peers)
    slots = vals_ref.shape[1]
    block = vals_ref.shape[2]
    rows_dev = feat_ref.shape[1]
    size = rows_dev // chunks
    layers = sections
    pslot = 3 - 2 * odd
    fsrc = 4 - 4 * odd
    fdst = 3 - 2 * odd
    other = 4 * odd
    fslot = 1 + 2 * odd

    own_copy = pltpu.make_async_copy(feat_ref.at[batch], win.at[0, REACH], local_sem.at[0])
    own_copy.start()
    vals_copy = pltpu.make_async_copy(
        vals_ref.at[batch], tiles.at[pl.ds(0, slots)], local_sem.at[1]
    )
    vals_copy.start()
    w_copies = [
        pltpu.make_async_copy(ref.at[0], wbuf.at[section, i], local_sem.at[2 + i])
        for i, ref in enumerate((ws_ref, wn_ref))
    ]
    for copy in w_copies:
        copy.start()

    barrier = pltpu.get_barrier_semaphore()
    for near in (peer, up, down):
        pl.semaphore_signal(barrier, inc=1, device_id=(section, near), device_id_type=MESH)
    for k in range(1, sections):
        pl.semaphore_signal(
            barrier, inc=1, device_id=(lax.rem(section + k, sections), me), device_id_type=MESH
        )
    pl.semaphore_wait(barrier, 3 + sections - 1)

    def halo(par, c, way):
        rows = pl.ds(c * size, size)
        target, slot = ((up, 0), (down, 4), (peer, 1 + 2 * odd))[way]
        return pltpu.make_async_remote_copy(
            src_ref=win.at[par, REACH, rows],
            dst_ref=win.at[par, slot, rows],
            send_sem=send_sem.at[way, c],
            recv_sem=recv_sem.at[par, slot, c],
            device_id=(section, target),
            device_id_type=MESH,
        )

    def forward(par, c):
        rows = pl.ds(c * size, size)
        return pltpu.make_async_remote_copy(
            src_ref=win.at[par, fsrc, rows],
            dst_ref=win.at[par, fdst, rows],
            send_sem=fwd_sem.at[c],
            recv_sem=recv_sem.at[par, fdst, c],
            device_id=(section, peer),
            device_id_type=MESH,
        )

    def arrival(par, slot, c):
        rows = pl.ds(c * size, size)
        return pltpu.make_async_remote_copy(
            src_ref=win.at[par, slot, rows],
            dst_ref=win.at[par, slot, rows],
            send_sem=fwd_sem.at[c],
            recv_sem=recv_sem.at[par, slot, c],
            device_id=(section, peer),
            device_id_type=MESH,
        )

    def weight(k, i):
        ref = (ws_ref, wn_ref)[i]
        return pltpu.make_async_remote_copy(
            src_ref=ref.at[0],
            dst_ref=wbuf.at[section, i],
            send_sem=wsend_sem.at[k, i],
            recv_sem=wrecv_sem.at[section, i],
            device_id=(lax.rem(section + k, sections), me),
            device_id_type=MESH,
        )

    def weight_arrival(layer, i):
        return pltpu.make_async_remote_copy(
            src_ref=wbuf.at[layer, i],
            dst_ref=wbuf.at[layer, i],
            send_sem=wsend_sem.at[0, i],
            recv_sem=wrecv_sem.at[layer, i],
            device_id=(lax.rem(section + 1, sections), me),
            device_id_type=MESH,
        )

    def output_local(par, c):
        rows = pl.ds(c * size, size)
        return pltpu.make_async_copy(
            win.at[par, REACH, rows], out_ref.at[0, batch, rows], osend_sem.at[c]
        )

    def output_remote(layer, par, c):
        rows = pl.ds(c * size, size)
        return pltpu.make_async_remote_copy(
            src_ref=win.at[par, REACH, rows],
            dst_ref=out_ref.at[0, batch, rows],
            send_sem=osend_sem.at[c],
            recv_sem=orecv_sem.at[batch, c],
            device_id=(layer, me),
            device_id_type=MESH,
        )

    def output_arrival(m, c):
        rows = pl.ds(c * size, size)
        return pltpu.make_async_remote_copy(
            src_ref=win.at[0, REACH, rows],
            dst_ref=out_ref.at[0, m, rows],
            send_sem=osend_sem.at[c],
            recv_sem=orecv_sem.at[m, c],
            device_id=(lax.rem(section + 1, sections), me),
            device_id_type=MESH,
        )

    def is_sender(layer):
        return jnp.logical_and(
            layer != section, lax.rem(layer, group) == lax.rem(section, group)
        )

    own_copy.wait()
    for c in range(chunks):
        for way in range(3):
            halo(0, c, way).start()
    for k in range(1, sections):
        for i in range(2):
            weight(k, i).start()

    tiles[slots] = jnp.zeros((block, block), tiles.dtype)
    for r in range(blocks):
        span = pl.ds(r * block, block)
        degrees = deg_ref[:, span].astype(jnp.float32)
        chosen = lax.broadcasted_iota(jnp.int32, degrees.shape, 0) == batch
        degree = jnp.sum(jnp.where(chosen, degrees, 0.0), axis=0, keepdims=True)
        column = jnp.broadcast_to(1.0 / degree, (block, block)).T
        for half in range(rdeg.shape[1] // block):
            rdeg[span, pl.ds(half * block, block)] = column
    for copy in w_copies:
        copy.wait()
    vals_copy.wait()

    def place(s, carry):
        for r in range(blocks):
            for c in range(blocks):
                slot = slot_ref[batch, r * (SPAN * blocks) + s * blocks + c]
                slab[s, r * block:(r + 1) * block, c * block:(c + 1) * block] = tiles[slot]
        return carry

    lax.fori_loop(0, SPAN, place, 0)

    def dot(a, b):
        return jnp.dot(a, b, preferred_element_type=jnp.float32)

    def layer_step(layer, carry):
        par = lax.rem(layer, 2)
        nxt = 1 - par

        @pl.when(layer != section)
        def _():
            for i in range(2):
                weight_arrival(layer, i).wait_recv()

        own_part[...] = dot(win[par, REACH], wbuf[layer, 0])
        acc[...] = dot(slab[REACH], win[par, REACH])
        for c in range(chunks):
            arrival(par, fsrc, c).wait_recv()
            forward(par, c).start()
        for c in range(chunks):
            arrival(par, pslot, c).wait_recv()
        acc[...] += dot(slab[pslot], win[par, pslot])
        acc[...] += dot(slab[fsrc], win[par, fsrc])
        for c in range(chunks):
            arrival(par, other, c).wait_recv()
        acc[...] += dot(slab[other], win[par, other])
        for c in range(chunks):
            arrival(par, fslot, c).wait_recv()
        acc[...] += dot(slab[fslot], win[par, fslot])

        for c in range(chunks):
            for way in range(3):
                halo(par, c, way).wait_send()
            forward(par, c).wait_send()

        @pl.when(layer - 1 == section)
        def _():
            for c in range(chunks):
                output_local(par, c).wait()

        @pl.when(jnp.logical_and(layer >= 1, is_sender(layer - 1)))
        def _():
            for c in range(chunks):
                output_remote(layer - 1, par, c).wait_send()

        for c in range(chunks):
            rows = pl.ds(c * size, size)
            mean = (acc[rows, :] * rdeg[rows, :]).astype(jnp.bfloat16)
            combined = own_part[rows, :] + dot(mean, wbuf[layer, 1])
            active = jnp.maximum(combined, 0.0)
            scale = lax.rsqrt(jnp.mean(active * active, axis=-1, keepdims=True) + 1e-05)
            win[nxt, REACH, rows, :] = (active * scale).astype(jnp.bfloat16)

            @pl.when(layer < layers - 1)
            def _():
                for way in range(3):
                    halo(nxt, c, way).start()

            @pl.when(layer == section)
            def _():
                output_local(nxt, c).start()

            @pl.when(is_sender(layer))
            def _():
                output_remote(layer, nxt, c).start()

        return carry

    lax.fori_loop(0, layers, layer_step, 0)

    last = layers - 1

    @pl.when(section == last)
    def _():
        for c in range(chunks):
            output_local(layers % 2, c).wait()

    @pl.when(is_sender(last))
    def _():
        for c in range(chunks):
            output_remote(last, layers % 2, c).wait_send()

    for m in range(batches):

        @pl.when(batch != m)
        def _():
            for c in range(chunks):
                output_arrival(m, c).wait_recv()

    for k in range(1, sections):
        for i in range(2):
            weight(k, i).wait_send()


def slot_table(tile_rows, tile_cols, tile_count, blocks_dev, blk_count):
    slot_total = tile_rows.shape[1]
    band = SPAN * blocks_dev
    blk_index = lax.axis_index("blk")
    shifted = jnp.mod(tile_cols // blocks_dev - blk_index + REACH, blk_count)
    column_local = shifted * blocks_dev + jnp.mod(tile_cols, blocks_dev)
    row_local = tile_rows - blk_index * blocks_dev
    target = row_local * band + column_local
    ids = jnp.arange(slot_total, dtype=jnp.int32)
    target = jnp.where(ids[None, :] < tile_count, target, -1)
    places = jnp.arange(blocks_dev * band, dtype=jnp.int32)
    hit = target[:, None, :] == places[None, :, None]
    return jnp.min(jnp.where(hit, ids[None, None, :], slot_total), axis=2)


def body(
    features, tile_values, tile_rows, tile_cols, tile_count, degrees, self_weight, neighbour_weight
):
    batches, rows_dev, width = features.shape
    slots, block = tile_values.shape[1], tile_values.shape[2]
    blocks = rows_dev // block
    sections = lax.axis_size("section")
    peers = lax.axis_size("blk")
    chunks = blocks
    table = slot_table(tile_rows, tile_cols, tile_count, blocks, peers)
    anywhere = pl.BlockSpec(memory_space=pl.ANY)
    hbm = pl.BlockSpec(memory_space=pltpu.HBM)
    dma = pltpu.SemaphoreType.DMA
    return pl.pallas_call(
        functools.partial(kernel, sections, peers, batches, blocks, chunks),
        out_shape=jax.ShapeDtypeStruct((1, batches, rows_dev, width), jnp.bfloat16),
        in_specs=[
            pl.BlockSpec(memory_space=pltpu.SMEM),
            pl.BlockSpec(memory_space=pltpu.VMEM),
            hbm, hbm, hbm, hbm,
        ],
        out_specs=anywhere,
        scratch_shapes=[
            pltpu.VMEM((slots + 1, block, block), jnp.bfloat16),
            pltpu.VMEM((SPAN, rows_dev, rows_dev), jnp.bfloat16),
            pltpu.VMEM((2, SPAN, rows_dev, width), jnp.bfloat16),
            pltpu.VMEM((sections, 2, width, width), jnp.bfloat16),
            pltpu.VMEM((rows_dev, width), jnp.float32),
            pltpu.VMEM((rows_dev, width), jnp.float32),
            pltpu.VMEM((rows_dev, width), jnp.float32),
            dma((4,)),
            dma((3, chunks)),
            dma((2, SPAN, chunks)),
            dma((chunks,)),
            dma((sections, 2)),
            dma((sections, 2)),
            dma((chunks,)),
            dma((batches, chunks)),
        ],
        compiler_params=pltpu.CompilerParams(
            collective_id=0, has_side_effects=True, vmem_limit_bytes=40 * 1024 * 1024
        ),
    )(table, degrees, features, tile_values, self_weight, neighbour_weight)


def solution(mesh):
    return jax.shard_map(
        body,
        mesh=mesh,
        in_specs=(
            P(None, "blk", None),
            P(None, "blk", None, None),
            P(None, "blk"),
            P(None, "blk"),
            P(None, "blk"),
            P(None, "blk"),
            P("section", None, None),
            P("section", None, None),
        ),
        out_specs=P("section", None, "blk", None),
        check_vma=False,
    )
```

```python
import functools

import jax
import jax.numpy as jnp
from jax import lax
from jax.experimental import pallas as pl
from jax.experimental.pallas import tpu as pltpu
from jax.sharding import PartitionSpec as P

REACH = 2
SPAN = 2 * REACH + 1
MESH = pl.DeviceIdType.MESH


def kernel(
    sections, peers, batches, blocks, chunks,
    slot_ref, deg_ref, feat_ref, vals_ref, ws_ref, wn_ref, out_ref,
    tiles, slab, win, wbuf, acc, own_part, rdeg,
    local_sem, send_sem, recv_sem, fwd_sem, wsend_sem, wrecv_sem, osend_sem, orecv_sem, turn_sem,
):
    section = lax.axis_index("section")
    me = lax.axis_index("blk")
    group = sections // batches
    batch = section // group
    late = lax.rem(section, 2)
    odd = lax.rem(me, 2)
    peer = me + 1 - 2 * odd
    up = lax.rem(me + 2, peers)
    down = lax.rem(me + peers - 2, peers)
    slots = vals_ref.shape[1]
    block = vals_ref.shape[2]
    rows_dev = feat_ref.shape[1]
    size = rows_dev // chunks
    layers = sections
    pslot = 3 - 2 * odd
    fsrc = 4 - 4 * odd
    fdst = 3 - 2 * odd
    other = 4 * odd
    fslot = 1 + 2 * odd

    own_copy = pltpu.make_async_copy(feat_ref.at[batch], win.at[0, REACH], local_sem.at[0])
    own_copy.start()
    vals_copy = pltpu.make_async_copy(
        vals_ref.at[batch], tiles.at[pl.ds(0, slots)], local_sem.at[1]
    )
    vals_copy.start()
    w_copies = [
        pltpu.make_async_copy(ref.at[0], wbuf.at[section, i], local_sem.at[2 + i])
        for i, ref in enumerate((ws_ref, wn_ref))
    ]
    for copy in w_copies:
        copy.start()

    barrier = pltpu.get_barrier_semaphore()
    for near in (peer, up, down):
        pl.semaphore_signal(barrier, inc=1, device_id=(section, near), device_id_type=MESH)
    for k in range(1, sections):
        pl.semaphore_signal(
            barrier, inc=1, device_id=(lax.rem(section + k, sections), me), device_id_type=MESH
        )
    pl.semaphore_wait(barrier, 3 + sections - 1)

    def halo(par, c, way):
        rows = pl.ds(c * size, size)
        target, slot = ((up, 0), (down, 4), (peer, 1 + 2 * odd))[way]
        return pltpu.make_async_remote_copy(
            src_ref=win.at[par, REACH, rows],
            dst_ref=win.at[par, slot, rows],
            send_sem=send_sem.at[way, c],
            recv_sem=recv_sem.at[par, slot, c],
            device_id=(section, target),
            device_id_type=MESH,
        )

    def forward(par, c):
        rows = pl.ds(c * size, size)
        return pltpu.make_async_remote_copy(
            src_ref=win.at[par, fsrc, rows],
            dst_ref=win.at[par, fdst, rows],
            send_sem=fwd_sem.at[c],
            recv_sem=recv_sem.at[par, fdst, c],
            device_id=(section, peer),
            device_id_type=MESH,
        )

    def arrival(par, slot, c):
        rows = pl.ds(c * size, size)
        return pltpu.make_async_remote_copy(
            src_ref=win.at[par, slot, rows],
            dst_ref=win.at[par, slot, rows],
            send_sem=fwd_sem.at[c],
            recv_sem=recv_sem.at[par, slot, c],
            device_id=(section, peer),
            device_id_type=MESH,
        )

    def weight(k, i):
        ref = (ws_ref, wn_ref)[i]
        return pltpu.make_async_remote_copy(
            src_ref=ref.at[0],
            dst_ref=wbuf.at[section, i],
            send_sem=wsend_sem.at[k, i],
            recv_sem=wrecv_sem.at[section, i],
            device_id=(lax.rem(section + k, sections), me),
            device_id_type=MESH,
        )

    def weight_arrival(layer, i):
        return pltpu.make_async_remote_copy(
            src_ref=wbuf.at[layer, i],
            dst_ref=wbuf.at[layer, i],
            send_sem=wsend_sem.at[0, i],
            recv_sem=wrecv_sem.at[layer, i],
            device_id=(lax.rem(section + 1, sections), me),
            device_id_type=MESH,
        )

    def output_local(par, c):
        rows = pl.ds(c * size, size)
        return pltpu.make_async_copy(
            win.at[par, REACH, rows], out_ref.at[0, batch, rows], osend_sem.at[c]
        )

    def output_remote(layer, par, c):
        rows = pl.ds(c * size, size)
        return pltpu.make_async_remote_copy(
            src_ref=win.at[par, REACH, rows],
            dst_ref=out_ref.at[0, batch, rows],
            send_sem=osend_sem.at[c],
            recv_sem=orecv_sem.at[batch, c],
            device_id=(layer, me),
            device_id_type=MESH,
        )

    def output_arrival(m, c):
        rows = pl.ds(c * size, size)
        return pltpu.make_async_remote_copy(
            src_ref=win.at[0, REACH, rows],
            dst_ref=out_ref.at[0, m, rows],
            send_sem=osend_sem.at[c],
            recv_sem=orecv_sem.at[m, c],
            device_id=(lax.rem(section + 1, sections), me),
            device_id_type=MESH,
        )

    def is_sender(layer):
        return jnp.logical_and(
            layer != section, lax.rem(layer, group) == lax.rem(section, group)
        )

    own_copy.wait()

    @pl.when(late == 0)
    def _():
        for c in range(chunks):
            for way in range(3):
                halo(0, c, way).start()

    for k in range(1, sections):
        for i in range(2):
            weight(k, i).start()

    tiles[slots] = jnp.zeros((block, block), tiles.dtype)
    for r in range(blocks):
        span = pl.ds(r * block, block)
        degrees = deg_ref[:, span].astype(jnp.float32)
        chosen = lax.broadcasted_iota(jnp.int32, degrees.shape, 0) == batch
        degree = jnp.sum(jnp.where(chosen, degrees, 0.0), axis=0, keepdims=True)
        column = jnp.broadcast_to(1.0 / degree, (block, block)).T
        for half in range(rdeg.shape[1] // block):
            rdeg[span, pl.ds(half * block, block)] = column
    for copy in w_copies:
        copy.wait()
    vals_copy.wait()

    def place(s, carry):
        for r in range(blocks):
            for c in range(blocks):
                slot = slot_ref[batch, r * (SPAN * blocks) + s * blocks + c]
                slab[s, r * block:(r + 1) * block, c * block:(c + 1) * block] = tiles[slot]
        return carry

    lax.fori_loop(0, SPAN, place, 0)

    @pl.when(late == 1)
    def _():
        pl.semaphore_wait(turn_sem, 1)
        for c in range(chunks):
            for way in range(3):
                halo(0, c, way).start()

    def dot(a, b):
        return jnp.dot(a, b, preferred_element_type=jnp.float32)

    def layer_step(layer, carry):
        par = lax.rem(layer, 2)
        nxt = 1 - par

        @pl.when(layer != section)
        def _():
            for i in range(2):
                weight_arrival(layer, i).wait_recv()

        own_part[...] = dot(win[par, REACH], wbuf[layer, 0])
        acc[...] = dot(slab[REACH], win[par, REACH])
        for c in range(chunks):
            arrival(par, fsrc, c).wait_recv()
            forward(par, c).start()
        for c in range(chunks):
            arrival(par, pslot, c).wait_recv()
        acc[...] += dot(slab[pslot], win[par, pslot])
        acc[...] += dot(slab[fsrc], win[par, fsrc])
        for c in range(chunks):
            arrival(par, other, c).wait_recv()

        @pl.when(jnp.logical_and(layer == 0, late == 0))
        def _():
            pl.semaphore_signal(
                turn_sem, inc=1, device_id=(section + 1, me), device_id_type=MESH
            )

        acc[...] += dot(slab[other], win[par, other])
        for c in range(chunks):
            arrival(par, fslot, c).wait_recv()
        acc[...] += dot(slab[fslot], win[par, fslot])

        for c in range(chunks):
            for way in range(3):
                halo(par, c, way).wait_send()
            forward(par, c).wait_send()

        @pl.when(layer - 1 == section)
        def _():
            for c in range(chunks):
                output_local(par, c).wait()

        @pl.when(jnp.logical_and(layer >= 1, is_sender(layer - 1)))
        def _():
            for c in range(chunks):
                output_remote(layer - 1, par, c).wait_send()

        for c in range(chunks):
            rows = pl.ds(c * size, size)
            mean = (acc[rows, :] * rdeg[rows, :]).astype(jnp.bfloat16)
            combined = own_part[rows, :] + dot(mean, wbuf[layer, 1])
            active = jnp.maximum(combined, 0.0)
            scale = lax.rsqrt(jnp.mean(active * active, axis=-1, keepdims=True) + 1e-05)
            win[nxt, REACH, rows, :] = (active * scale).astype(jnp.bfloat16)

            @pl.when(layer < layers - 1)
            def _():
                for way in range(3):
                    halo(nxt, c, way).start()

            @pl.when(layer == section)
            def _():
                output_local(nxt, c).start()

            @pl.when(is_sender(layer))
            def _():
                output_remote(layer, nxt, c).start()

        return carry

    lax.fori_loop(0, layers, layer_step, 0)

    last = layers - 1

    @pl.when(section == last)
    def _():
        for c in range(chunks):
            output_local(layers % 2, c).wait()

    @pl.when(is_sender(last))
    def _():
        for c in range(chunks):
            output_remote(last, layers % 2, c).wait_send()

    for m in range(batches):

        @pl.when(batch != m)
        def _():
            for c in range(chunks):
                output_arrival(m, c).wait_recv()

    for k in range(1, sections):
        for i in range(2):
            weight(k, i).wait_send()


def slot_table(tile_rows, tile_cols, tile_count, blocks_dev, blk_count):
    slot_total = tile_rows.shape[1]
    band = SPAN * blocks_dev
    blk_index = lax.axis_index("blk")
    shifted = jnp.mod(tile_cols // blocks_dev - blk_index + REACH, blk_count)
    column_local = shifted * blocks_dev + jnp.mod(tile_cols, blocks_dev)
    row_local = tile_rows - blk_index * blocks_dev
    target = row_local * band + column_local
    ids = jnp.arange(slot_total, dtype=jnp.int32)
    target = jnp.where(ids[None, :] < tile_count, target, -1)
    places = jnp.arange(blocks_dev * band, dtype=jnp.int32)
    hit = target[:, None, :] == places[None, :, None]
    return jnp.min(jnp.where(hit, ids[None, None, :], slot_total), axis=2)


def body(
    features, tile_values, tile_rows, tile_cols, tile_count, degrees, self_weight, neighbour_weight
):
    batches, rows_dev, width = features.shape
    slots, block = tile_values.shape[1], tile_values.shape[2]
    blocks = rows_dev // block
    sections = lax.axis_size("section")
    peers = lax.axis_size("blk")
    chunks = blocks
    table = slot_table(tile_rows, tile_cols, tile_count, blocks, peers)
    anywhere = pl.BlockSpec(memory_space=pl.ANY)
    hbm = pl.BlockSpec(memory_space=pltpu.HBM)
    dma = pltpu.SemaphoreType.DMA
    return pl.pallas_call(
        functools.partial(kernel, sections, peers, batches, blocks, chunks),
        out_shape=jax.ShapeDtypeStruct((1, batches, rows_dev, width), jnp.bfloat16),
        in_specs=[
            pl.BlockSpec(memory_space=pltpu.SMEM),
            pl.BlockSpec(memory_space=pltpu.VMEM),
            hbm, hbm, hbm, hbm,
        ],
        out_specs=anywhere,
        scratch_shapes=[
            pltpu.VMEM((slots + 1, block, block), jnp.bfloat16),
            pltpu.VMEM((SPAN, rows_dev, rows_dev), jnp.bfloat16),
            pltpu.VMEM((2, SPAN, rows_dev, width), jnp.bfloat16),
            pltpu.VMEM((sections, 2, width, width), jnp.bfloat16),
            pltpu.VMEM((rows_dev, width), jnp.float32),
            pltpu.VMEM((rows_dev, width), jnp.float32),
            pltpu.VMEM((rows_dev, width), jnp.float32),
            dma((4,)),
            dma((3, chunks)),
            dma((2, SPAN, chunks)),
            dma((chunks,)),
            dma((sections, 2)),
            dma((sections, 2)),
            dma((chunks,)),
            dma((batches, chunks)),
            pltpu.SemaphoreType.REGULAR,
        ],
        compiler_params=pltpu.CompilerParams(
            collective_id=0, has_side_effects=True, vmem_limit_bytes=60 * 1024 * 1024
        ),
    )(table, degrees, features, tile_values, self_weight, neighbour_weight)


def solution(mesh):
    return jax.shard_map(
        body,
        mesh=mesh,
        in_specs=(
            P(None, "blk", None),
            P(None, "blk", None, None),
            P(None, "blk"),
            P(None, "blk"),
            P(None, "blk"),
            P(None, "blk"),
            P("section", None, None),
            P("section", None, None),
        ),
        out_specs=P("section", None, "blk", None),
        check_vma=False,
    )
```

```python
import functools

import jax
import jax.numpy as jnp
from jax import lax
from jax.experimental import pallas as pl
from jax.experimental.pallas import tpu as pltpu
from jax.sharding import PartitionSpec as P

REACH = 2
SPAN = 2 * REACH + 1
MESH = pl.DeviceIdType.MESH


def kernel(
    sections, peers, batches, blocks, chunks,
    slot_ref, deg_ref, feat_ref, vals_ref, ws_ref, wn_ref, out_ref,
    tiles, slab, win, wbuf, acc, own_part, rdeg,
    local_sem, send_sem, recv_sem, fwd_sem, wsend_sem, wrecv_sem, osend_sem, orecv_sem, turn_sem,
):
    section = lax.axis_index("section")
    me = lax.axis_index("blk")
    group = sections // batches
    batch = section // group
    late = lax.rem(section, 2)
    odd = lax.rem(me, 2)
    peer = me + 1 - 2 * odd
    up = lax.rem(me + 2, peers)
    down = lax.rem(me + peers - 2, peers)
    slots = vals_ref.shape[1]
    block = vals_ref.shape[2]
    rows_dev = feat_ref.shape[1]
    size = rows_dev // chunks
    layers = sections
    first = jnp.where(odd == 1, up, down)
    second = jnp.where(odd == 1, down, up)
    pslot = 3 - 2 * odd
    fsrc = 4 - 4 * odd
    fdst = 3 - 2 * odd
    other = 4 * odd
    fslot = 1 + 2 * odd

    own_copy = pltpu.make_async_copy(feat_ref.at[batch], win.at[0, REACH], local_sem.at[0])
    own_copy.start()
    vals_copy = pltpu.make_async_copy(
        vals_ref.at[batch], tiles.at[pl.ds(0, slots)], local_sem.at[1]
    )
    vals_copy.start()
    w_copies = [
        pltpu.make_async_copy(ref.at[0], wbuf.at[section, i], local_sem.at[2 + i])
        for i, ref in enumerate((ws_ref, wn_ref))
    ]
    for copy in w_copies:
        copy.start()

    barrier = pltpu.get_barrier_semaphore()
    for near in (peer, up, down):
        pl.semaphore_signal(barrier, inc=1, device_id=(section, near), device_id_type=MESH)
    for k in range(1, sections):
        pl.semaphore_signal(
            barrier, inc=1, device_id=(lax.rem(section + k, sections), me), device_id_type=MESH
        )
    pl.semaphore_wait(barrier, 3 + sections - 1)

    def halo(par, c, way, source=None):
        rows = pl.ds(c * size, size)
        source = win.at[par, REACH] if source is None else source
        target, slot = ((first, fsrc), (second, other), (peer, 1 + 2 * odd))[way]
        return pltpu.make_async_remote_copy(
            src_ref=source.at[rows],
            dst_ref=win.at[par, slot, rows],
            send_sem=send_sem.at[par, way, c],
            recv_sem=recv_sem.at[par, slot, c],
            device_id=(section, target),
            device_id_type=MESH,
        )

    def forward(par, c):
        rows = pl.ds(c * size, size)
        return pltpu.make_async_remote_copy(
            src_ref=win.at[par, fsrc, rows],
            dst_ref=win.at[par, fdst, rows],
            send_sem=fwd_sem.at[c],
            recv_sem=recv_sem.at[par, fdst, c],
            device_id=(section, peer),
            device_id_type=MESH,
        )

    def arrival(par, slot, c):
        rows = pl.ds(c * size, size)
        return pltpu.make_async_remote_copy(
            src_ref=win.at[par, slot, rows],
            dst_ref=win.at[par, slot, rows],
            send_sem=fwd_sem.at[c],
            recv_sem=recv_sem.at[par, slot, c],
            device_id=(section, peer),
            device_id_type=MESH,
        )

    def weight(k, i):
        ref = (ws_ref, wn_ref)[i]
        return pltpu.make_async_remote_copy(
            src_ref=ref.at[0],
            dst_ref=wbuf.at[section, i],
            send_sem=wsend_sem.at[k, i],
            recv_sem=wrecv_sem.at[section, i],
            device_id=(lax.rem(section + k, sections), me),
            device_id_type=MESH,
        )

    def weight_arrival(layer, i):
        return pltpu.make_async_remote_copy(
            src_ref=wbuf.at[layer, i],
            dst_ref=wbuf.at[layer, i],
            send_sem=wsend_sem.at[0, i],
            recv_sem=wrecv_sem.at[layer, i],
            device_id=(lax.rem(section + 1, sections), me),
            device_id_type=MESH,
        )

    def output_local(par, c):
        rows = pl.ds(c * size, size)
        return pltpu.make_async_copy(
            win.at[par, REACH, rows], out_ref.at[0, batch, rows], osend_sem.at[par, c]
        )

    def output_remote(layer, par, c):
        rows = pl.ds(c * size, size)
        return pltpu.make_async_remote_copy(
            src_ref=win.at[par, REACH, rows],
            dst_ref=out_ref.at[0, batch, rows],
            send_sem=osend_sem.at[par, c],
            recv_sem=orecv_sem.at[batch, c],
            device_id=(layer, me),
            device_id_type=MESH,
        )

    def output_arrival(m, c):
        rows = pl.ds(c * size, size)
        return pltpu.make_async_remote_copy(
            src_ref=win.at[0, REACH, rows],
            dst_ref=out_ref.at[0, m, rows],
            send_sem=osend_sem.at[0, c],
            recv_sem=orecv_sem.at[m, c],
            device_id=(lax.rem(section + 1, sections), me),
            device_id_type=MESH,
        )

    def is_sender(layer):
        return jnp.logical_and(
            layer != section, lax.rem(layer, group) == lax.rem(section, group)
        )

    def send_weights():
        for k in range(1, sections):
            for i in range(2):
                weight(k, i).start()

    @pl.when(late == 0)
    def _():
        for c in range(chunks):
            for way in range(3):
                halo(0, c, way, feat_ref.at[batch]).start()
        send_weights()

    tiles[slots] = jnp.zeros((block, block), tiles.dtype)
    for r in range(blocks):
        span = pl.ds(r * block, block)
        degrees = deg_ref[:, span].astype(jnp.float32)
        chosen = lax.broadcasted_iota(jnp.int32, degrees.shape, 0) == batch
        degree = jnp.sum(jnp.where(chosen, degrees, 0.0), axis=0, keepdims=True)
        column = jnp.broadcast_to(1.0 / degree, (block, block)).T
        for half in range(rdeg.shape[1] // block):
            rdeg[span, pl.ds(half * block, block)] = column
    for copy in w_copies:
        copy.wait()
    own_copy.wait()
    vals_copy.wait()

    def place(s, carry):
        for r in range(blocks):
            for c in range(blocks):
                slot = slot_ref[batch, r * (SPAN * blocks) + s * blocks + c]
                slab[s, r * block:(r + 1) * block, c * block:(c + 1) * block] = tiles[slot]
        return carry

    lax.fori_loop(0, SPAN, place, 0)

    @pl.when(late == 1)
    def _():
        pl.semaphore_wait(turn_sem, 1)
        for c in range(chunks):
            for way in range(3):
                halo(0, c, way, feat_ref.at[batch]).start()
        send_weights()

    def dot(a, b):
        return jnp.dot(a, b, preferred_element_type=jnp.float32)

    def layer_step(layer, carry):
        par = lax.rem(layer, 2)
        nxt = 1 - par

        acc[...] = dot(slab[REACH], win[par, REACH])
        for c in range(chunks):
            arrival(par, fsrc, c).wait_recv()
            forward(par, c).start()
        for c in range(chunks):
            arrival(par, pslot, c).wait_recv()
        @pl.when(jnp.logical_and(layer == 0, late == 0))
        def _():
            pl.semaphore_signal(
                turn_sem, inc=1, device_id=(section + 1, me), device_id_type=MESH
            )

        acc[...] += dot(slab[pslot], win[par, pslot])
        acc[...] += dot(slab[fsrc], win[par, fsrc])
        for c in range(chunks):
            arrival(par, other, c).wait_recv()

        acc[...] += dot(slab[other], win[par, other])
        @pl.when(layer != section)
        def _():
            for i in range(2):
                weight_arrival(layer, i).wait_recv()

        own_part[...] = dot(win[par, REACH], wbuf[layer, 0])

        for c in range(chunks):
            arrival(par, fslot, c).wait_recv()

        for c in range(chunks):
            forward(par, c).wait_send()

        for c in range(chunks):
            rows = pl.ds(c * size, size)
            total = acc[rows, :] + dot(slab[fslot, rows, :], win[par, fslot])
            mean = (total * rdeg[rows, :]).astype(jnp.bfloat16)
            combined = own_part[rows, :] + dot(mean, wbuf[layer, 1])
            active = jnp.maximum(combined, 0.0)
            scale = lax.rsqrt(jnp.mean(active * active, axis=-1, keepdims=True) + 1e-05)
            win[nxt, REACH, rows, :] = (active * scale).astype(jnp.bfloat16)

            @pl.when(layer < layers - 1)
            def _():
                for way in range(3):
                    halo(nxt, c, way).start()

            @pl.when(layer == section)
            def _():
                output_local(nxt, c).start()

            @pl.when(is_sender(layer))
            def _():
                output_remote(layer, nxt, c).start()

        for c in range(chunks):
            for way in range(3):
                halo(par, c, way).wait_send()

        @pl.when(layer - 1 == section)
        def _():
            for c in range(chunks):
                output_local(par, c).wait()

        @pl.when(jnp.logical_and(layer >= 1, is_sender(layer - 1)))
        def _():
            for c in range(chunks):
                output_remote(layer - 1, par, c).wait_send()

        return carry

    lax.fori_loop(0, layers, layer_step, 0)

    last = layers - 1

    @pl.when(section == last)
    def _():
        for c in range(chunks):
            output_local(layers % 2, c).wait()

    @pl.when(is_sender(last))
    def _():
        for c in range(chunks):
            output_remote(last, layers % 2, c).wait_send()

    for m in range(batches):

        @pl.when(batch != m)
        def _():
            for c in range(chunks):
                output_arrival(m, c).wait_recv()

    for k in range(1, sections):
        for i in range(2):
            weight(k, i).wait_send()


def slot_table(tile_rows, tile_cols, tile_count, blocks_dev, blk_count):
    slot_total = tile_rows.shape[1]
    band = SPAN * blocks_dev
    blk_index = lax.axis_index("blk")
    shifted = jnp.mod(tile_cols // blocks_dev - blk_index + REACH, blk_count)
    column_local = shifted * blocks_dev + jnp.mod(tile_cols, blocks_dev)
    row_local = tile_rows - blk_index * blocks_dev
    target = row_local * band + column_local
    ids = jnp.arange(slot_total, dtype=jnp.int32)
    target = jnp.where(ids[None, :] < tile_count, target, -1)
    places = jnp.arange(blocks_dev * band, dtype=jnp.int32)
    hit = target[:, None, :] == places[None, :, None]
    return jnp.min(jnp.where(hit, ids[None, None, :], slot_total), axis=2)


def body(
    features, tile_values, tile_rows, tile_cols, tile_count, degrees, self_weight, neighbour_weight
):
    batches, rows_dev, width = features.shape
    slots, block = tile_values.shape[1], tile_values.shape[2]
    blocks = rows_dev // block
    sections = lax.axis_size("section")
    peers = lax.axis_size("blk")
    chunks = blocks
    table = slot_table(tile_rows, tile_cols, tile_count, blocks, peers)
    anywhere = pl.BlockSpec(memory_space=pl.ANY)
    hbm = pl.BlockSpec(memory_space=pltpu.HBM)
    dma = pltpu.SemaphoreType.DMA
    return pl.pallas_call(
        functools.partial(kernel, sections, peers, batches, blocks, chunks),
        out_shape=jax.ShapeDtypeStruct((1, batches, rows_dev, width), jnp.bfloat16),
        in_specs=[
            pl.BlockSpec(memory_space=pltpu.SMEM),
            pl.BlockSpec(memory_space=pltpu.VMEM),
            hbm, hbm, hbm, hbm,
        ],
        out_specs=anywhere,
        scratch_shapes=[
            pltpu.VMEM((slots + 1, block, block), jnp.bfloat16),
            pltpu.VMEM((SPAN, rows_dev, rows_dev), jnp.bfloat16),
            pltpu.VMEM((2, SPAN, rows_dev, width), jnp.bfloat16),
            pltpu.VMEM((sections, 2, width, width), jnp.bfloat16),
            pltpu.VMEM((rows_dev, width), jnp.float32),
            pltpu.VMEM((rows_dev, width), jnp.float32),
            pltpu.VMEM((rows_dev, width), jnp.float32),
            dma((4,)),
            dma((2, 3, chunks)),
            dma((2, SPAN, chunks)),
            dma((chunks,)),
            dma((sections, 2)),
            dma((sections, 2)),
            dma((2, chunks)),
            dma((batches, chunks)),
            pltpu.SemaphoreType.REGULAR,
        ],
        compiler_params=pltpu.CompilerParams(
            collective_id=0, has_side_effects=True, vmem_limit_bytes=60 * 1024 * 1024
        ),
    )(table, degrees, features, tile_values, self_weight, neighbour_weight)


def solution(mesh):
    return jax.shard_map(
        body,
        mesh=mesh,
        in_specs=(
            P(None, "blk", None),
            P(None, "blk", None, None),
            P(None, "blk"),
            P(None, "blk"),
            P(None, "blk"),
            P(None, "blk"),
            P("section", None, None),
            P("section", None, None),
        ),
        out_specs=P("section", None, "blk", None),
        check_vma=False,
    )
```
